32 devices in a mesh: expert: 4 (over x, core), dp: 8 (over z, y).
Axes of the slice: x: 2, y: 2, z: 4, core: 2. Of those that a mesh axis runs over, the one named last changes fastest.
Arguments:
- tokens: bfloat16 [4096, 2048], P(('expert', 'dp')), may hold values from -6 to 6
- grad_out: bfloat16 [4096, 2048], P(('expert', 'dp')), may hold values from -6 to 6
- combine: bfloat16 [4096, 8], P(('expert', 'dp')), may hold values from 0.099609375 to 1
- expert_ids: int32 [4096, 8], P(('expert', 'dp')), may hold values from 0 to 31, as said below
- slots: int32 [4096, 8], P(('expert', 'dp')), may hold values from 0 to 39, as said below
- w_gate: bfloat16 [32, 2048, 768], P(('expert', 'dp')), may hold values from -0.125 to 0.125
- w_up: bfloat16 [32, 2048, 768], P(('expert', 'dp')), may hold values from -0.125 to 0.125
- w_down: bfloat16 [32, 768, 2048], P(('expert', 'dp')), may hold values from -0.21875 to 0.21875
Outputs:
- input_grad: bfloat16 [4096, 2048], P(('expert', 'dp'))
- prob_grad: bfloat16 [4096, 8], P(('expert', 'dp'))
- gate_wgrad: bfloat16 [32, 2048, 768], P(('expert', 'dp'))
- up_wgrad: bfloat16 [32, 2048, 768], P(('expert', 'dp'))
- down_wgrad: bfloat16 [32, 768, 2048], P(('expert', 'dp'))
The draws below stay inside these ranges and needn't reach their ends.
Inputs may be any that keep to these rules, and one draw needn't show every extreme that they name: `expert_ids`: each token names 8 different experts. In the rows of one device no expert is named by more than 40 rows, and in every device's rows some expert is named by exactly 40 rows; every expert is named by some row of every device. Within the rows of one device, the rows that name the same expert hold different slots.
All inputs are finite; a program needn't handle non-finite values.
Results may differ from the reference program's by a relative error of at most 0.0064.
Values may be sent and summed in bfloat16 or wider, within the bound.
A program may use at most 128 MiB of HBM per device.

```python
import math
import jax
import jax.numpy as jnp
from jax import lax

D = 2048
FF = 768
TOP = 8
TOK_DEV = 128
EXPERTS = 32
CAP = 40
TOKENS = 4096


def routing(key):
    folded = jax.random.fold_in(key, 11)
    average = TOK_DEV * TOP // EXPERTS
    headroom = CAP - average

    def one_block(block_key):
        subkeys = jax.random.split(block_key, 5)
        pairing = jax.random.permutation(subkeys[0], EXPERTS)
        amounts = jax.random.randint(subkeys[1], (EXPERTS // 2,), 0, headroom + 1).astype(jnp.int32)
        amounts = amounts.at[0].set(headroom)
        loads_per = jnp.full((EXPERTS,), average, jnp.int32)
        loads_per = loads_per.at[pairing[0::2]].add(amounts).at[pairing[1::2]].add(-amounts)
        run_ends = jnp.cumsum(loads_per).astype(jnp.int32)
        run_starts = run_ends - loads_per
        position = jnp.arange(TOK_DEV * TOP, dtype=jnp.int32)
        owners = jnp.sum((position[:, None] >= run_ends[None, :]).astype(jnp.int32), axis=1)
        within = position - run_starts[owners]
        offsets = jax.random.randint(subkeys[2], (EXPERTS,), 0, CAP).astype(jnp.int32)
        slot_of = (within + offsets[owners]) % CAP
        expert_of = owners.reshape(TOP, TOK_DEV).T
        slot_of = slot_of.reshape(TOP, TOK_DEV).T
        perm_rows = jax.random.permutation(subkeys[3], TOK_DEV)
        expert_of = expert_of[perm_rows]
        slot_of = slot_of[perm_rows]
        scores = jax.random.randint(subkeys[4], (TOK_DEV, TOP), 0, 1 << 20).astype(jnp.int32) * TOP
        scores = scores + jnp.arange(TOP, dtype=jnp.int32)[None, :]
        shuffle = jnp.argsort(scores, axis=1, stable=True)
        return (jnp.take_along_axis(expert_of, shuffle, 1), jnp.take_along_axis(slot_of, shuffle, 1))
    expert_of, slot_of = jax.vmap(one_block)(jax.random.split(folded, EXPERTS))
    return (expert_of.reshape(TOKENS, TOP).astype(jnp.int32), slot_of.reshape(TOKENS, TOP).astype(jnp.int32))


def draw_expert_ids(key, part):
    return routing(key)[0]


def draw_slots(key, part):
    return routing(key)[1]


def level_of(own_key, dims, cuts, low, largest):
    gain, own = 1.0, jax.random.fold_in(own_key, 6)
    for axis_at, parts in cuts:
        heights = jnp.exp(jax.random.uniform(jax.random.fold_in(own, axis_at), (parts,), jnp.float32, low / len(cuts), largest / len(cuts)))
        gain = gain * jnp.repeat(heights, dims[axis_at] // parts).reshape([-1 if axis == axis_at else 1 for axis in range(len(dims))])
    return gain


def noise(own_key, extent, scale, reach, cuts=(), held_as=jnp.bfloat16):
    result = jax.random.normal(own_key, extent, jnp.float32) * scale
    if len(cuts) > 0:
        result = level_of(own_key, extent, cuts, -0.22, 0.18) * result
    return jnp.clip(result, min=-reach, max=reach).astype(held_as)


def setup_inputs(seed: int = 0) -> dict:
    splits = jax.random.split(jax.random.key(seed), 9)
    return {
        "tokens": noise(splits[0], (TOKENS, D), 1.0, 6.0, ((0, 32),)),
        "grad_out": noise(splits[1], (TOKENS, D), 1.0, 6.0, ((0, 32),)),
        "combine": jnp.clip(jnp.exp(math.log(1.0) - 2.306499 * jax.random.uniform(splits[2], (TOKENS, TOP), jnp.float32) ** level_of(splits[2], (TOKENS, TOP), ((0, 32),), -0.2, 0.2)), 0.099609375, 1.0).astype(jnp.bfloat16),
        "expert_ids": draw_expert_ids(jax.random.fold_in(splits[8], 71), 0),
        "slots": draw_slots(jax.random.fold_in(splits[8], 71), 0),
        "w_gate": noise(splits[5], (EXPERTS, D, FF), D ** -0.5, 0.125, ((0, 32),)),
        "w_up": noise(splits[6], (EXPERTS, D, FF), D ** -0.5, 0.125, ((0, 32),)),
        "w_down": noise(splits[7], (EXPERTS, FF, D), FF ** -0.5, 0.21875, ((0, 32),)),
    }


def expert_grads(rows_x, rows_dy, rows_w, gate_weight, up_weight, down_weight):
    gate_act = jnp.dot(rows_x, gate_weight, preferred_element_type=jnp.float32)
    up_act = jnp.dot(rows_x, up_weight, preferred_element_type=jnp.float32)
    sig_gate = jax.nn.sigmoid(gate_act)
    active = gate_act * sig_gate
    hidden = (active * up_act).astype(jnp.bfloat16)
    output = jnp.dot(hidden, down_weight, preferred_element_type=jnp.float32)
    row_prob = jnp.sum(rows_dy.astype(jnp.float32) * output, axis=1).astype(jnp.bfloat16)
    scaled = (rows_w.astype(jnp.float32)[:, None] * rows_dy.astype(jnp.float32)).astype(jnp.bfloat16)
    down_grad = lax.dot_general(hidden, scaled, (((0,), (0,)), ((), ())), preferred_element_type=jnp.float32).astype(jnp.bfloat16)
    dhidden = lax.dot_general(scaled, down_weight, (((1,), (1,)), ((), ())), preferred_element_type=jnp.float32)
    dgate = (dhidden * up_act * sig_gate * (1.0 + gate_act * (1.0 - sig_gate))).astype(jnp.bfloat16)
    dup_act = (dhidden * active).astype(jnp.bfloat16)
    gate_grad = lax.dot_general(rows_x, dgate, (((0,), (0,)), ((), ())), preferred_element_type=jnp.float32).astype(jnp.bfloat16)
    up_grad = lax.dot_general(rows_x, dup_act, (((0,), (0,)), ((), ())), preferred_element_type=jnp.float32).astype(jnp.bfloat16)
    row_grad = lax.dot_general(dgate, gate_weight, (((1,), (1,)), ((), ())), preferred_element_type=jnp.float32)
    row_grad = row_grad + lax.dot_general(dup_act, up_weight, (((1,), (1,)), ((), ())), preferred_element_type=jnp.float32)
    return row_grad.astype(jnp.bfloat16), row_prob, gate_grad, up_grad, down_grad


def reference(tokens, grad_out, combine, expert_ids, slots, w_gate, w_up, w_down):
    total = TOKENS * TOP
    flat_index = jnp.arange(total, dtype=jnp.int32)
    source_dev = (flat_index // TOP) // TOK_DEV
    column_at = (source_dev * CAP + slots.reshape(-1)).astype(jnp.int32)
    row_table = jnp.full((EXPERTS, EXPERTS * CAP), total, jnp.int32)
    row_table = row_table.at[expert_ids.reshape(-1).astype(jnp.int32), column_at].set(flat_index)
    pad_x = jnp.concatenate([tokens, jnp.zeros((1, D), tokens.dtype)], axis=0)
    pad_dy = jnp.concatenate([grad_out, jnp.zeros((1, D), grad_out.dtype)], axis=0)
    pad_w = jnp.concatenate([combine.reshape(-1), jnp.zeros((1,), combine.dtype)], axis=0)

    def per_expert(running, inputs):
        summed, prob_acc = running
        row_index, gate_weight, up_weight, down_weight = inputs
        owners = (row_index // TOP).astype(jnp.int32)
        results = expert_grads(pad_x[owners], pad_dy[owners], pad_w[row_index], gate_weight, up_weight, down_weight)
        summed = summed.at[owners].add(results[0].astype(jnp.float32))
        prob_acc = prob_acc.at[row_index].set(results[1])
        return (summed, prob_acc), (results[2], results[3], results[4])

    initial = (jnp.zeros((TOKENS + 1, D), jnp.float32), jnp.zeros((total + 1,), jnp.bfloat16))
    (summed, prob_acc), weight_grads = lax.scan(per_expert, initial, (row_table, w_gate, w_up, w_down))
    input_grad = summed[:TOKENS].astype(jnp.bfloat16)
    prob_grad = prob_acc[:total].reshape(TOKENS, TOP)
    return input_grad, prob_grad, weight_grads[0], weight_grads[1], weight_grads[2]
```

```python
import jax
import jax.numpy as jnp
from jax import lax
from jax.sharding import Mesh, PartitionSpec as P

DISPATCH_PARTS = 2
RETURN_PARTS = 2
F32 = jnp.float32
BF16 = jnp.bfloat16
PLANE = ("expert", "y")
ALL = ("expert", "z", "y")


def dot_t(a, b, a_dim, b_dim):
    return lax.dot_general(a, b, (((a_dim,), (b_dim,)), ((), ())), preferred_element_type=F32)


def shift_z(block, distance):
    planes = lax.axis_size("z")
    return lax.ppermute(block, "z", [(i, (i + distance) % planes) for i in range(planes)])


def plane_exchange(rows):
    groups = lax.axis_size("expert") * lax.axis_size("y")
    split = rows.reshape(groups, rows.shape[0] // groups, rows.shape[1])
    out = lax.all_to_all(split, PLANE, split_axis=0, concat_axis=0, tiled=True)
    return out.reshape(rows.shape)


def by_distance(table, axis):
    planes = lax.axis_size("z")
    flipped = jnp.flip(table, axis)
    twice = jnp.concatenate([flipped, flipped], axis)
    return lax.dynamic_slice_in_dim(twice, planes - 1 - lax.axis_index("z"), planes, axis)


def on_device(tokens, grad_out, combine, expert_ids, slots, w_gate, w_up, w_down):
    w_gate, w_up, w_down = w_gate[0], w_up[0], w_down[0]
    tok_rows, width = tokens.shape
    top = expert_ids.shape[1]
    n_e, n_z, n_y = lax.axis_size("expert"), lax.axis_size("z"), lax.axis_size("y")
    experts = n_e * n_z * n_y
    cap = tok_rows * top * 5 // (4 * experts)
    groups = n_e * n_y
    my_z = lax.axis_index("z")

    code = expert_ids * cap + slots
    codes = [code] + [shift_z(code, d) for d in range(1, n_z)]
    column_code = jnp.stack(codes)
    group = jnp.arange(groups, dtype=jnp.int32)
    target = (group // n_y) * (n_z * n_y) + my_z * n_y + group % n_y
    local = column_code[None] - (target * cap)[:, None, None, None]
    hit = (local >= 0) & (local < cap)
    distance = jnp.arange(n_z, dtype=jnp.int32)[None, :, None, None]
    place = jnp.sum(jnp.where(hit, local + distance * cap + 1, 0), axis=3) - 1
    place = place.reshape(groups, 1, n_z * tok_rows)
    seat = jnp.arange(n_z * cap, dtype=jnp.int32)[None, :, None]
    pick = (place == seat).astype(BF16).reshape(groups * n_z * cap, n_z * tok_rows)

    every = jnp.arange(experts, dtype=jnp.int32)[:, None, None]
    own = expert_ids[None] == every
    slot_of = jnp.sum(jnp.where(own, slots[None] + 1, 0), axis=2) - 1
    weight_of = jnp.sum(jnp.where(own, combine[None].astype(F32), 0.0), axis=2)
    seats = jnp.arange(cap, dtype=jnp.int32)[None, :, None]
    spread_w = jnp.sum(jnp.where(slot_of[:, None] == seats, weight_of[:, None], 0.0), axis=2)
    recv_w = lax.all_to_all(spread_w.astype(BF16), ALL, split_axis=0, concat_axis=0, tiled=True)
    rows_w = by_distance(recv_w.reshape(n_e, n_z, n_y, cap).transpose(0, 2, 1, 3), 2)
    rows_w = rows_w.reshape(-1, 1).astype(F32)

    def dispatch(block):
        part = width // DISPATCH_PARTS
        out = []
        for i in range(DISPATCH_PARTS):
            mine = block[:, i * part : (i + 1) * part]
            column = jnp.concatenate([mine] + [shift_z(mine, d) for d in range(1, n_z)], 0)
            out.append(plane_exchange(dot_t(pick, column, 1, 0).astype(BF16)))
        return jnp.concatenate(out, 1)

    rows_x = dispatch(tokens)
    rows_dy = dispatch(grad_out)

    gate = dot_t(rows_x, w_gate, 1, 0)
    up = dot_t(rows_x, w_up, 1, 0)
    sig = jax.nn.sigmoid(gate)
    active = gate * sig
    hidden = (active * up).astype(BF16)
    back = dot_t(rows_dy, w_down, 1, 1)
    row_prob = jnp.sum(hidden.astype(F32) * back, axis=1).astype(BF16)
    dhidden = rows_w * back
    dgate = (dhidden * up * sig * (1.0 + gate * (1.0 - sig))).astype(BF16)
    dup = (dhidden * active).astype(BF16)

    part = width // RETURN_PARTS
    grads = []
    for i in range(RETURN_PARTS):
        cols = slice(i * part, (i + 1) * part)
        row_grad = (dot_t(dgate, w_gate[cols], 1, 1) + dot_t(dup, w_up[cols], 1, 1)).astype(BF16)
        partial = dot_t(pick, plane_exchange(row_grad), 0, 0).astype(BF16)
        partial = partial.reshape(n_z, tok_rows, part)
        total = partial[0].astype(F32)
        for d in range(1, n_z):
            total = total + shift_z(partial[d], n_z - d).astype(F32)
        grads.append(total.astype(BF16))
    input_grad = jnp.concatenate(grads, 1)

    prob = by_distance(row_prob.reshape(n_e, n_y, n_z, cap), 2).transpose(0, 2, 1, 3)
    back_prob = lax.all_to_all(
        prob.reshape(experts, cap), ALL, split_axis=0, concat_axis=0, tiled=True
    )
    here = code[:, :, None] == jnp.arange(experts * cap, dtype=jnp.int32)
    prob_grad = jnp.sum(jnp.where(here, back_prob.reshape(-1).astype(F32), 0.0), axis=2)

    scaled = (rows_w * rows_dy.astype(F32)).astype(BF16)
    gate_wgrad = dot_t(rows_x, dgate, 0, 0).astype(BF16)
    up_wgrad = dot_t(rows_x, dup, 0, 0).astype(BF16)
    down_wgrad = dot_t(hidden, scaled, 0, 0).astype(BF16)
    return input_grad, prob_grad.astype(BF16), gate_wgrad[None], up_wgrad[None], down_wgrad[None]


def solution(mesh):
    n_e, n_dp = mesh.shape["expert"], mesh.shape["dp"]
    n_z = 4 if n_dp % 4 == 0 else 1
    cube = Mesh(mesh.devices.reshape(n_e, n_z, n_dp // n_z), ALL)
    flat, deep = P(ALL, None), P(ALL, None, None)
    return jax.shard_map(
        on_device,
        mesh=cube,
        in_specs=(flat,) * 5 + (deep,) * 3,
        out_specs=(flat, flat, deep, deep, deep),
        check_vma=False,
    )
```

```python
import jax
import jax.numpy as jnp
from jax import lax
from jax.sharding import Mesh, PartitionSpec as P

F32 = jnp.float32
BF16 = jnp.bfloat16
PLANE = ("expert", "y")
ALL = ("expert", "z", "y")


def dot_t(a, b, a_dim, b_dim):
    return lax.dot_general(a, b, (((a_dim,), (b_dim,)), ((), ())), preferred_element_type=F32)


def shift_z(block, distance):
    planes = lax.axis_size("z")
    return lax.ppermute(block, "z", [(i, (i + distance) % planes) for i in range(planes)])


def batches_of(planes):
    if planes <= 2:
        return [(d,) for d in range(planes)]
    return [(0,), (1,), tuple(range(2, planes))]


def plane_exchange(rows):
    groups = lax.axis_size("expert") * lax.axis_size("y")
    split = rows.reshape(groups, rows.shape[0] // groups, rows.shape[1])
    out = lax.all_to_all(split, PLANE, split_axis=0, concat_axis=0, tiled=True)
    return out.reshape(rows.shape)


def by_distance(table, axis):
    planes = lax.axis_size("z")
    flipped = jnp.flip(table, axis)
    twice = jnp.concatenate([flipped, flipped], axis)
    return lax.dynamic_slice_in_dim(twice, planes - 1 - lax.axis_index("z"), planes, axis)


def on_device(tokens, grad_out, combine, expert_ids, slots, w_gate, w_up, w_down):
    w_gate, w_up, w_down = w_gate[0], w_up[0], w_down[0]
    tok_rows, width = tokens.shape
    top = expert_ids.shape[1]
    n_e, n_z, n_y = lax.axis_size("expert"), lax.axis_size("z"), lax.axis_size("y")
    experts = n_e * n_z * n_y
    cap = tok_rows * top * 5 // (4 * experts)
    groups = n_e * n_y
    my_z = lax.axis_index("z")

    code = expert_ids * cap + slots
    codes = jnp.stack([code] + [shift_z(code, d) for d in range(1, n_z)])
    group = jnp.arange(groups, dtype=jnp.int32)
    target = (group // n_y) * (n_z * n_y) + my_z * n_y + group % n_y

    def pick_rows(members):
        local = codes[members[0] : members[-1] + 1][None] - (target * cap)[:, None, None, None]
        hit = (local >= 0) & (local < cap)
        offset = jnp.arange(len(members), dtype=jnp.int32)[None, :, None, None] * cap
        place = jnp.sum(jnp.where(hit, local + offset + 1, 0), axis=3) - 1
        place = place.reshape(groups, 1, len(members) * tok_rows)
        seat = jnp.arange(len(members) * cap, dtype=jnp.int32)[None, :, None]
        return (place == seat).astype(BF16).reshape(-1, len(members) * tok_rows)

    batches = batches_of(n_z)
    picks = [pick_rows(m) for m in batches]

    every = jnp.arange(experts, dtype=jnp.int32)[:, None, None]
    own = expert_ids[None] == every
    slot_of = jnp.sum(jnp.where(own, slots[None] + 1, 0), axis=2) - 1
    weight_of = jnp.sum(jnp.where(own, combine[None].astype(F32), 0.0), axis=2)
    seats = jnp.arange(cap, dtype=jnp.int32)[None, :, None]
    spread_w = jnp.sum(jnp.where(slot_of[:, None] == seats, weight_of[:, None], 0.0), axis=2)
    recv_w = lax.all_to_all(spread_w.astype(BF16), ALL, split_axis=0, concat_axis=0, tiled=True)
    by_dist = by_distance(recv_w.reshape(n_e, n_z, n_y, cap).transpose(0, 2, 1, 3), 2)
    rows_w = [by_dist[:, :, m[0] : m[-1] + 1].reshape(-1, 1).astype(F32) for m in batches]

    both = jnp.concatenate([tokens, grad_out], 1)
    own_rows = plane_exchange(dot_t(picks[0], both, 1, 0).astype(BF16))
    xs, dys = [own_rows[:, :width]], [own_rows[:, width:]]
    for mine, rows in ((tokens, xs), (grad_out, dys)):
        moved = {d: shift_z(mine, d) for d in range(1, n_z)}
        for members, pick in zip(batches[1:], picks[1:]):
            column = jnp.concatenate([moved[d] for d in members], 0)
            rows.append(plane_exchange(dot_t(pick, column, 1, 0).astype(BF16)))

    fronts = []
    for x in xs:
        gate = dot_t(x, w_gate, 1, 0)
        up = dot_t(x, w_up, 1, 0)
        fronts.append((gate, up, jax.nn.sigmoid(gate)))

    hiddens, probs, dgates, dups, scales, sends = [], [], [], [], [], []
    for (gate, up, sig), dy, w in zip(fronts, dys, rows_w):
        active = gate * sig
        hidden = (active * up).astype(BF16)
        back = dot_t(dy, w_down, 1, 1)
        probs.append(jnp.sum(hidden.astype(F32) * back, axis=1).astype(BF16))
        dhidden = w * back
        dgate = (dhidden * up * sig * (1.0 + gate * (1.0 - sig))).astype(BF16)
        dup = (dhidden * active).astype(BF16)
        sends.append((dot_t(dgate, w_gate, 1, 1) + dot_t(dup, w_up, 1, 1)).astype(BF16))
        scales.append((w * dy.astype(F32)).astype(BF16))
        hiddens.append(hidden)
        dgates.append(dgate)
        dups.append(dup)

    total = 0.0
    for at in list(range(1, len(batches))) + [0]:
        members = batches[at]
        partial = dot_t(picks[at], plane_exchange(sends[at]), 0, 0)
        for i, d in enumerate(members):
            piece = partial[i * tok_rows : (i + 1) * tok_rows]
            if d:
                piece = shift_z(piece.astype(BF16), n_z - d).astype(F32)
            total = total + piece
    input_grad = total.astype(BF16)

    prob = jnp.concatenate(
        [p.reshape(n_e, n_y, len(m), cap) for p, m in zip(probs, batches)], axis=2
    )
    prob = by_distance(prob, 2).transpose(0, 2, 1, 3)
    back_prob = lax.all_to_all(
        prob.reshape(experts, cap), ALL, split_axis=0, concat_axis=0, tiled=True
    )
    here = code[:, :, None] == jnp.arange(experts * cap, dtype=jnp.int32)
    prob_grad = jnp.sum(jnp.where(here, back_prob.reshape(-1).astype(F32), 0.0), axis=2)

    rows_x, dgate, dup = (jnp.concatenate(v, 0) for v in (xs, dgates, dups))
    gate_wgrad = dot_t(rows_x, dgate, 0, 0).astype(BF16)
    up_wgrad = dot_t(rows_x, dup, 0, 0).astype(BF16)
    down_wgrad = dot_t(jnp.concatenate(hiddens, 0), jnp.concatenate(scales, 0), 0, 0).astype(BF16)
    return input_grad, prob_grad.astype(BF16), gate_wgrad[None], up_wgrad[None], down_wgrad[None]


def solution(mesh):
    n_e, n_dp = mesh.shape["expert"], mesh.shape["dp"]
    n_z = 4 if n_dp % 4 == 0 else 1
    cube = Mesh(mesh.devices.reshape(n_e, n_z, n_dp // n_z), ALL)
    flat, deep = P(ALL, None), P(ALL, None, None)
    return jax.shard_map(
        on_device,
        mesh=cube,
        in_specs=(flat,) * 5 + (deep,) * 3,
        out_specs=(flat, flat, deep, deep, deep),
        check_vma=False,
    )
```

```python
import jax
import jax.numpy as jnp
from jax import lax
from jax.sharding import Mesh, PartitionSpec as P

RETURN_PARTS = 2
F32 = jnp.float32
BF16 = jnp.bfloat16
PLANE = ("expert", "y")
ALL = ("expert", "z", "y")


def dot_t(a, b, a_dim, b_dim):
    return lax.dot_general(a, b, (((a_dim,), (b_dim,)), ((), ())), preferred_element_type=F32)


def shift_z(block, distance):
    planes = lax.axis_size("z")
    return lax.ppermute(block, "z", [(i, (i + distance) % planes) for i in range(planes)])


def after(value, other):
    return lax.optimization_barrier((value, other))[0]


def plane_exchange(rows):
    groups = lax.axis_size("expert") * lax.axis_size("y")
    split = rows.reshape(groups, rows.shape[0] // groups, rows.shape[1])
    out = lax.all_to_all(split, PLANE, split_axis=0, concat_axis=0, tiled=True)
    return out.reshape(rows.shape)


def by_distance(table, axis):
    planes = lax.axis_size("z")
    flipped = jnp.flip(table, axis)
    twice = jnp.concatenate([flipped, flipped], axis)
    return lax.dynamic_slice_in_dim(twice, planes - 1 - lax.axis_index("z"), planes, axis)


def on_device(tokens, grad_out, combine, expert_ids, slots, w_gate, w_up, w_down):
    w_gate, w_up, w_down = w_gate[0], w_up[0], w_down[0]
    tok_rows, width = tokens.shape
    top = expert_ids.shape[1]
    n_e, n_z, n_y = lax.axis_size("expert"), lax.axis_size("z"), lax.axis_size("y")
    experts = n_e * n_z * n_y
    cap = tok_rows * top * 5 // (4 * experts)
    groups = n_e * n_y
    my_z = lax.axis_index("z")

    code = expert_ids * cap + slots
    codes = jnp.stack([code] + [shift_z(code, d) for d in range(1, n_z)])
    group = jnp.arange(groups, dtype=jnp.int32)
    target = (group // n_y) * (n_z * n_y) + my_z * n_y + group % n_y

    def pick_rows(members):
        local = codes[members[0] : members[-1] + 1][None] - (target * cap)[:, None, None, None]
        hit = (local >= 0) & (local < cap)
        offset = jnp.arange(len(members), dtype=jnp.int32)[None, :, None, None] * cap
        place = jnp.sum(jnp.where(hit, local + offset + 1, 0), axis=3) - 1
        place = place.reshape(groups, 1, len(members) * tok_rows)
        seat = jnp.arange(len(members) * cap, dtype=jnp.int32)[None, :, None]
        return (place == seat).astype(BF16).reshape(-1, len(members) * tok_rows)

    batches = [(0,), tuple(range(1, n_z))]
    picks = [pick_rows(m) for m in batches]

    every = jnp.arange(experts, dtype=jnp.int32)[:, None, None]
    own = expert_ids[None] == every
    slot_of = jnp.sum(jnp.where(own, slots[None] + 1, 0), axis=2) - 1
    weight_of = jnp.sum(jnp.where(own, combine[None].astype(F32), 0.0), axis=2)
    seats = jnp.arange(cap, dtype=jnp.int32)[None, :, None]
    spread_w = jnp.sum(jnp.where(slot_of[:, None] == seats, weight_of[:, None], 0.0), axis=2)
    recv_w = lax.all_to_all(spread_w.astype(BF16), ALL, split_axis=0, concat_axis=0, tiled=True)
    by_dist = by_distance(recv_w.reshape(n_e, n_z, n_y, cap).transpose(0, 2, 1, 3), 2)
    rows_w = [by_dist[:, :, m[0] : m[-1] + 1].reshape(-1, 1).astype(F32) for m in batches]

    def column_of(block):
        return [shift_z(block, d) for d in range(1, n_z)]

    both = jnp.concatenate([tokens, grad_out], 1)
    own_rows = plane_exchange(dot_t(picks[0], both, 1, 0).astype(BF16))
    x_column = column_of(tokens)
    dy_column = column_of(after(grad_out, x_column))
    x_rows = dot_t(picks[1], jnp.concatenate(x_column, 0), 1, 0).astype(BF16)
    x_rest = plane_exchange(after(x_rows, own_rows))
    dy_rows = dot_t(picks[1], jnp.concatenate(dy_column, 0), 1, 0).astype(BF16)
    dy_rest = plane_exchange(after(dy_rows, x_rest))
    xs, dys = [own_rows[:, :width], x_rest], [own_rows[:, width:], dy_rest]

    fronts = []
    for x in xs:
        gate = dot_t(x, w_gate, 1, 0)
        up = dot_t(x, w_up, 1, 0)
        fronts.append((gate, up, jax.nn.sigmoid(gate)))

    hiddens, probs, dgates, dups, scales = [], [], [], [], []
    for (gate, up, sig), dy, w in zip(fronts, dys, rows_w):
        active = gate * sig
        hidden = (active * up).astype(BF16)
        back = dot_t(dy, w_down, 1, 1)
        probs.append(jnp.sum(hidden.astype(F32) * back, axis=1).astype(BF16))
        dhidden = w * back
        dgate = (dhidden * up * sig * (1.0 + gate * (1.0 - sig))).astype(BF16)
        dup = (dhidden * active).astype(BF16)
        scales.append((w * dy.astype(F32)).astype(BF16))
        hiddens.append(hidden)
        dgates.append(dgate)
        dups.append(dup)

    def row_grad(at, cols):
        dots = dot_t(dgates[at], w_gate[cols], 1, 1) + dot_t(dups[at], w_up[cols], 1, 1)
        return dots.astype(BF16)

    part = width // RETURN_PARTS
    own_send = row_grad(0, slice(None))
    last, partials = None, []
    for i in range(RETURN_PARTS):
        send = row_grad(1, slice(i * part, (i + 1) * part))
        last = plane_exchange(send if last is None else after(send, last))
        partials.append(dot_t(picks[1], last, 0, 0).astype(BF16).reshape(n_z - 1, tok_rows, part))
    returned = [
        [shift_z(partial[d - 1], n_z - d) for d in range(1, n_z)] for partial in partials
    ]
    own_back = plane_exchange(after(own_send, last))
    own_partial = dot_t(picks[0], own_back, 0, 0)
    sums = [sum(p.astype(F32) for p in pieces) for pieces in returned]
    input_grad = (own_partial + jnp.concatenate(sums, 1)).astype(BF16)

    prob = jnp.concatenate(
        [p.reshape(n_e, n_y, len(m), cap) for p, m in zip(probs, batches)], axis=2
    )
    prob = by_distance(prob, 2).transpose(0, 2, 1, 3)
    back_prob = lax.all_to_all(
        after(prob.reshape(experts, cap), own_back), ALL, split_axis=0, concat_axis=0, tiled=True
    )
    here = code[:, :, None] == jnp.arange(experts * cap, dtype=jnp.int32)
    prob_grad = jnp.sum(jnp.where(here, back_prob.reshape(-1).astype(F32), 0.0), axis=2)

    rows_x, dgate, dup = (jnp.concatenate(v, 0) for v in (xs, dgates, dups))
    gate_wgrad = dot_t(rows_x, dgate, 0, 0).astype(BF16)
    up_wgrad = dot_t(rows_x, dup, 0, 0).astype(BF16)
    hidden = after(jnp.concatenate(hiddens, 0), partials[0])
    down_wgrad = dot_t(hidden, jnp.concatenate(scales, 0), 0, 0).astype(BF16)
    return input_grad, prob_grad.astype(BF16), gate_wgrad[None], up_wgrad[None], down_wgrad[None]


def solution(mesh):
    n_e, n_dp = mesh.shape["expert"], mesh.shape["dp"]
    n_z = 4 if n_dp % 4 == 0 else 1
    cube = Mesh(mesh.devices.reshape(n_e, n_z, n_dp // n_z), ALL)
    flat, deep = P(ALL, None), P(ALL, None, None)
    return jax.shard_map(
        on_device,
        mesh=cube,
        in_specs=(flat,) * 5 + (deep,) * 3,
        out_specs=(flat, flat, deep, deep, deep),
        check_vma=False,
    )
```
